256 devices in a mesh: dp: 8 (over z), tensor: 32 (over y, x, core).
Axes of the slice: x: 4, y: 4, z: 8, core: 2. Of those that a mesh axis runs over, the one named last changes fastest.
Arguments:
- gradient: bfloat16 [8, 4096, 14336], P('dp', None, 'tensor'), may hold values from -12 to 12
- feedback: bfloat16 [8, 4096, 14336], P('dp', None, 'tensor'), may hold values from -6 to 6
- right_prior: float32 [14336, 8], P('tensor'), may hold values from -6 to 6
Outputs:
- update: bfloat16 [4096, 14336], P('dp', 'tensor')
- new_feedback: bfloat16 [8, 4096, 14336], P('dp', None, 'tensor')
- right_next: float32 [14336, 8], P('tensor')
The draws below stay inside these ranges and needn't reach their ends.
All inputs are finite; a program needn't handle non-finite values.
Results may differ from the reference program's by a relative error of at most 0.0011.
Values sent between devices are 32-bit elements; how exact they have to be, the bound alone decides.
No kernel may reach another device: no remote copies, remote signals or barrier semaphores. Data moves between devices by JAX's collectives and lax.ppermute only.
A program may use at most 64 MiB of HBM per device.

```python
import jax
import jax.numpy as jnp
from jax import lax

D = 4096
FF = 14336
RANK = 8
REPLICAS = 8
N_DP = 8


def block_levels(key, dims, split, low, top_value):
    def one(axis_at, parts):
        heights = jax.random.uniform(jax.random.fold_in(jax.random.fold_in(key, 6), axis_at), (parts,), jnp.float32, low / len(split), top_value / len(split))
        return jnp.repeat(jnp.exp(heights), dims[axis_at] // parts).reshape((-1,) + (1,) * (len(dims) - axis_at - 1))

    loudness = one(*split[0])
    for cut in split[1:]:
        loudness = loudness * one(*cut)
    return loudness


def scatter_about(stream_key, dims, spread, reach, shards=(), kind=jnp.bfloat16):
    level = block_levels(stream_key, dims, shards, -0.22, 0.18) if shards else 1.0
    array = jax.random.normal(stream_key, dims, jnp.float32) * spread * level
    return jnp.minimum(jnp.maximum(array, -reach), reach).astype(kind)


def setup_inputs(seed: int = 0) -> dict:
    key_of = jax.random.split(jax.random.key(seed), 4)
    return {
        "gradient": scatter_about(key_of[0], (REPLICAS, D, FF), 2.0, 12.0, ((0, 8), (2, 32))),
        "feedback": scatter_about(key_of[1], (REPLICAS, D, FF), 1.0, 6.0, ((0, 8), (2, 32))),
        "right_prior": scatter_about(key_of[2], (FF, RANK), 1.0, 6.0, ((0, 32),), jnp.float32),
    }


def orthonormal(matrix):
    basis = []
    for column in range(RANK):
        vector = matrix[:, column]
        for earlier in basis:
            vector = vector - jnp.dot(earlier, vector, precision=lax.Precision.HIGHEST) * earlier
        vector = vector * lax.rsqrt(jnp.sum(vector * vector) + 1e-06)
        basis.append(vector)
    return jnp.stack(basis, axis=1)

def reference(gradient, feedback, right_prior):

    def left_term(pair):
        corrected = pair[0].astype(jnp.float32) + pair[1].astype(jnp.float32)
        return jnp.dot(corrected, right_prior, precision=lax.Precision.HIGHEST)
    left_sum = lax.optimization_barrier(jnp.sum(lax.map(left_term, (gradient, feedback)), axis=0))
    basis = orthonormal(left_sum)

    def right_term(pair):
        corrected = pair[0].astype(jnp.float32) + pair[1].astype(jnp.float32)
        return jnp.dot(corrected.T, basis, precision=lax.Precision.HIGHEST)
    right_next = lax.optimization_barrier(jnp.sum(lax.map(right_term, (gradient, feedback)), axis=0)) / N_DP
    rebuilt = jnp.dot(basis, right_next.T, precision=lax.Precision.HIGHEST)

    def residue(pair):
        corrected = pair[0].astype(jnp.float32) + pair[1].astype(jnp.float32)
        return (corrected - rebuilt).astype(jnp.bfloat16)
    new_feedback = lax.map(residue, (gradient, feedback))
    return (rebuilt.astype(jnp.bfloat16), new_feedback, right_next)
```

```python
import functools

import jax
import jax.numpy as jnp
from jax import lax
from jax.experimental import pallas as pl
from jax.experimental.pallas import tpu as pltpu
from jax.sharding import PartitionSpec as P

RANK = 8
LANES = 128
CHUNK = 512
F32 = jnp.float32
BF16 = jnp.bfloat16
LAST_BOTH = (((1,), (1,)), ((), ()))


def thirds(x):
    high = x.astype(BF16).astype(F32)
    rest = x - high
    middle = rest.astype(BF16).astype(F32)
    low = (rest - middle).astype(BF16).astype(F32)
    return high, middle, low


def fetches(sources, targets, sems):
    chunks = []
    for step in range(sources[0].shape[1] // CHUNK):
        columns = pl.ds(step * CHUNK, CHUNK)
        chunk = []
        for which, (source, target) in enumerate(zip(sources, targets)):
            copy = pltpu.make_async_copy(source.at[:, columns], target.at[:, columns], sems.at[which, step])
            copy.start()
            chunk.append(copy)
        chunks.append(chunk)
    return chunks


def left_kernel(prior, gradient_far, feedback_far, left, gradient, feedback, sems):
    chunks = fetches((gradient_far, feedback_far), (gradient, feedback), sems)
    terms = jnp.concatenate(thirds(prior[...]), axis=0).astype(BF16)
    for step, chunk in enumerate(chunks):
        columns = pl.ds(step * CHUNK, CHUNK)
        for copy in chunk:
            copy.wait()
        total = jnp.dot(terms, gradient[:, columns], preferred_element_type=F32)
        total += jnp.dot(terms, feedback[:, columns], preferred_element_type=F32)
        total = total[:RANK] + total[RANK : 2 * RANK] + total[2 * RANK :]
        for tile in range(CHUNK // LANES):
            left[step * (CHUNK // LANES) + tile] = total[:, tile * LANES : (tile + 1) * LANES]


def right_kernel(left, gradient_far, feedback_far, basis, right, gradient, feedback, sems):
    chunks = fetches((gradient_far, feedback_far), (gradient, feedback), sems)
    value = left[...]
    rank_row = lax.broadcasted_iota(jnp.int32, (RANK, 1), 0)
    scale = jnp.zeros((RANK, 1), F32)
    for column in range(RANK):
        row = value[:, column : column + 1, :]
        inner = jnp.sum(jnp.sum(value * row, axis=0), axis=1, keepdims=True)
        inverse = lax.rsqrt(inner[column : column + 1] + 1e-06)
        scale = jnp.where(rank_row == column, inverse, scale)
        if column < RANK - 1:
            factor = jnp.where(rank_row > column, inner * inverse * inverse, 0.0)
            value = value - factor[None] * row
    value = value * scale[None]
    for tile in range(value.shape[0]):
        lanes = pl.ds(tile * LANES, LANES)
        high, middle, low = thirds(value[tile])
        basis[0:RANK, lanes] = high
        basis[RANK : 2 * RANK, lanes] = middle
        basis[2 * RANK : 3 * RANK, lanes] = low
    total = jnp.zeros((3 * RANK, gradient.shape[0]), F32)
    for step, chunk in enumerate(chunks):
        columns = pl.ds(step * CHUNK, CHUNK)
        for copy in chunk:
            copy.wait()
        terms = basis[:, columns].astype(BF16)
        total += lax.dot_general(terms, gradient[:, columns], LAST_BOTH, preferred_element_type=F32)
        total += lax.dot_general(terms, feedback[:, columns], LAST_BOTH, preferred_element_type=F32)
    right[...] = total[:RANK] + total[RANK : 2 * RANK] + total[2 * RANK :]


def rebuild_kernel(
    replicas, rights, basis, gradient_far, feedback_far, update, residue, right_next, gradient, feedback, staged, slab, in_sems, sems
):
    chunks = fetches((gradient_far, feedback_far), (gradient, feedback), in_sems)
    mine = lax.axis_index("dp")
    wide = gradient.shape[1]
    total = rights[0]
    for replica in range(1, replicas):
        total = total + rights[replica]
    right = total * (1.0 / replicas)
    right_next[...] = right
    first, second, third = thirds(right)
    lhs = jnp.concatenate((first, first, first, second, second, third), axis=0).astype(BF16)
    copies = []
    for step, chunk in enumerate(chunks):
        columns = pl.ds(step * CHUNK, CHUNK)
        one, two, three = (basis[RANK * k : RANK * (k + 1), columns] for k in range(3))
        rhs = jnp.concatenate((one, two, three, one, two, one), axis=0).astype(BF16)
        rebuilt = lax.dot_general(lhs, rhs, (((0,), (0,)), ((), ())), preferred_element_type=F32)
        for copy in chunk:
            copy.wait()
        corrected = gradient[:, columns].astype(F32) + feedback[:, columns].astype(F32)
        staged[:, columns] = (corrected - rebuilt).astype(BF16)
        copy = pltpu.make_async_copy(staged.at[:, columns], residue.at[:, columns], sems.at[step])
        copy.start()
        copies.append(copy)

        @pl.when(mine == step)
        def _():
            slab[...] = rebuilt.astype(BF16)

    copy = pltpu.make_async_copy(slab, update, sems.at[wide // CHUNK])
    copy.start()
    copies.append(copy)
    for copy in copies:
        copy.wait()


def shards(gradient, feedback, right_prior):
    gradient, feedback = gradient[0].T, feedback[0].T
    units, wide = gradient.shape
    replicas, parts = lax.axis_size("dp"), lax.axis_size("tensor")
    steps = wide // CHUNK
    vmem = pl.BlockSpec(memory_space=pltpu.VMEM)
    hbm = pl.BlockSpec(memory_space=pltpu.HBM)
    held = [pltpu.VMEM((units, wide), BF16)] * 2
    arrived = pltpu.SemaphoreType.DMA((2, steps))
    params = pltpu.CompilerParams(vmem_limit_bytes=24 * 2**20)
    with jax.named_scope("left"):
        left = pl.pallas_call(
            left_kernel,
            out_shape=jax.ShapeDtypeStruct((wide // LANES, RANK, LANES), F32),
            in_specs=[vmem, hbm, hbm],
            out_specs=vmem,
            scratch_shapes=[*held, arrived],
            compiler_params=params,
        )(right_prior.T, gradient, feedback)
    with jax.named_scope("left_sum"):
        piece = jnp.sum(lax.all_to_all(left, "tensor", 0, 0), axis=0)
        pieces = jnp.broadcast_to(piece[None], (replicas,) + piece.shape)
        piece = jnp.sum(lax.all_to_all(pieces, "dp", 0, 0), axis=0)
        pieces = jnp.broadcast_to(piece[None], (parts,) + piece.shape)
        left = lax.all_to_all(pieces, "tensor", 0, 0)
    with jax.named_scope("right"):
        basis, right = pl.pallas_call(
            right_kernel,
            out_shape=(jax.ShapeDtypeStruct((3 * RANK, wide), F32), jax.ShapeDtypeStruct((RANK, units), F32)),
            in_specs=[vmem, hbm, hbm],
            out_specs=[vmem, vmem],
            scratch_shapes=[*held, arrived],
            compiler_params=params,
        )(left, gradient, feedback)
    with jax.named_scope("right_sum"):
        rights = lax.all_to_all(jnp.broadcast_to(right[None], (replicas,) + right.shape), "dp", 0, 0)
    with jax.named_scope("rebuild"):
        update, residue, right_next = pl.pallas_call(
            functools.partial(rebuild_kernel, replicas),
            out_shape=(
                jax.ShapeDtypeStruct((units, CHUNK), BF16),
                jax.ShapeDtypeStruct((units, wide), BF16),
                jax.ShapeDtypeStruct((RANK, units), F32),
            ),
            in_specs=[vmem, vmem, hbm, hbm],
            out_specs=[hbm, hbm, vmem],
            scratch_shapes=[
                *held,
                pltpu.VMEM((units, wide), BF16),
                pltpu.VMEM((units, CHUNK), BF16),
                arrived,
                pltpu.SemaphoreType.DMA((steps + 1,)),
            ],
            compiler_params=params,
        )(rights, basis, gradient, feedback)
    return update.T, residue.T[None], right_next.T


def solution(mesh):
    placed = (P("dp", None, "tensor"), P("dp", None, "tensor"), P("tensor", None))
    return jax.shard_map(
        shards,
        mesh=mesh,
        in_specs=placed,
        out_specs=(P("dp", "tensor"), P("dp", None, "tensor"), P("tensor", None)),
        check_vma=False,
    )
```

```python
import functools

import jax
import jax.numpy as jnp
from jax import lax
from jax.experimental import pallas as pl
from jax.experimental.pallas import tpu as pltpu
from jax.sharding import PartitionSpec as P

RANK = 8
LANES = 128
CHUNK = 512
F32 = jnp.float32
BF16 = jnp.bfloat16
LAST_BOTH = (((1,), (1,)), ((), ()))


def thirds(x):
    high = x.astype(BF16).astype(F32)
    rest = x - high
    middle = rest.astype(BF16).astype(F32)
    low = (rest - middle).astype(BF16).astype(F32)
    return high, middle, low


def left_kernel(prior_far, gradient_far, feedback_far, left, gradient, feedback, prior, sems):
    steps = gradient.shape[1] // CHUNK
    prior_copy = pltpu.make_async_copy(prior_far, prior, sems.at[2, 0])
    prior_copy.start()
    chunks = []
    for step in range(steps):
        columns = pl.ds(step * CHUNK, CHUNK)
        chunk = []
        for which, (source, target) in enumerate(((gradient_far, gradient), (feedback_far, feedback))):
            copy = pltpu.make_async_copy(source.at[:, columns], target.at[:, columns], sems.at[which, step])
            copy.start()
            chunk.append(copy)
        chunks.append(chunk)
    prior_copy.wait()
    terms = jnp.concatenate(thirds(prior[...]), axis=0).astype(BF16)
    for step, chunk in enumerate(chunks):
        columns = pl.ds(step * CHUNK, CHUNK)
        for copy in chunk:
            copy.wait()
        total = jnp.dot(terms, gradient[:, columns], preferred_element_type=F32)
        total += jnp.dot(terms, feedback[:, columns], preferred_element_type=F32)
        total = total[:RANK] + total[RANK : 2 * RANK] + total[2 * RANK :]
        for tile in range(CHUNK // LANES):
            left[step * (CHUNK // LANES) + tile] = total[:, tile * LANES : (tile + 1) * LANES]


def spread_kernel(pieces, copies):
    total = pieces[0]
    for piece in range(1, pieces.shape[0]):
        total = total + pieces[piece]
    for copy in range(copies.shape[0]):
        copies[copy] = total


def right_kernel(left, gradient, feedback, basis, right):
    value = left[...]
    rank_row = lax.broadcasted_iota(jnp.int32, (RANK, 1), 0)
    scale = jnp.zeros((RANK, 1), F32)
    for column in range(RANK):
        row = value[:, column : column + 1, :]
        inner = jnp.sum(jnp.sum(value * row, axis=0), axis=1, keepdims=True)
        inverse = lax.rsqrt(inner[column : column + 1] + 1e-06)
        scale = jnp.where(rank_row == column, inverse, scale)
        if column < RANK - 1:
            factor = jnp.where(rank_row > column, inner * inverse * inverse, 0.0)
            value = value - factor[None] * row
    value = value * scale[None]
    for tile in range(value.shape[0]):
        lanes = pl.ds(tile * LANES, LANES)
        high, middle, low = thirds(value[tile])
        basis[0:RANK, lanes] = high
        basis[RANK : 2 * RANK, lanes] = middle
        basis[2 * RANK : 3 * RANK, lanes] = low
    terms = basis[...].astype(BF16)
    total = lax.dot_general(terms, gradient[...], LAST_BOTH, preferred_element_type=F32)
    total += lax.dot_general(terms, feedback[...], LAST_BOTH, preferred_element_type=F32)
    total = total[:RANK] + total[RANK : 2 * RANK] + total[2 * RANK :]
    for copy in range(right.shape[0]):
        right[copy] = total


def rebuild_kernel(
    replicas, rights, basis, gradient, feedback, update, residue, right_next, staged, slab, sems
):
    mine = lax.axis_index("dp")
    wide = gradient.shape[1]
    total = rights[0]
    for replica in range(1, replicas):
        total = total + rights[replica]
    right = total * (1.0 / replicas)
    right_next[...] = right
    first, second, third = thirds(right)
    lhs = jnp.concatenate((first, first, first, second, second, third), axis=0).astype(BF16)
    copies = []
    for step in range(wide // CHUNK):
        columns = pl.ds(step * CHUNK, CHUNK)
        one, two, three = (basis[RANK * k : RANK * (k + 1), columns] for k in range(3))
        rhs = jnp.concatenate((one, two, three, one, two, one), axis=0).astype(BF16)
        rebuilt = lax.dot_general(lhs, rhs, (((0,), (0,)), ((), ())), preferred_element_type=F32)
        corrected = gradient[:, columns].astype(F32) + feedback[:, columns].astype(F32)
        staged[:, columns] = (corrected - rebuilt).astype(BF16)
        copy = pltpu.make_async_copy(staged.at[:, columns], residue.at[:, columns], sems.at[step])
        copy.start()
        copies.append(copy)

        @pl.when(mine == step)
        def _():
            slab[...] = rebuilt.astype(BF16)

    copy = pltpu.make_async_copy(slab, update, sems.at[wide // CHUNK])
    copy.start()
    copies.append(copy)
    for copy in copies:
        copy.wait()


def shards(gradient, feedback, right_prior):
    gradient, feedback = gradient[0].T, feedback[0].T
    units, wide = gradient.shape
    replicas, parts = lax.axis_size("dp"), lax.axis_size("tensor")
    steps = wide // CHUNK
    vmem = pl.BlockSpec(memory_space=pltpu.VMEM)
    hbm = pl.BlockSpec(memory_space=pltpu.HBM)
    held = pltpu.VMEM((units, wide), BF16)
    params = pltpu.CompilerParams(vmem_limit_bytes=16 * 2**20)
    tile = (RANK, LANES)

    def spread(pieces, count):
        return pl.pallas_call(
            spread_kernel,
            out_shape=jax.ShapeDtypeStruct((count,) + tile, F32),
            in_specs=[vmem],
            out_specs=vmem,
            compiler_params=pltpu.CompilerParams(vmem_limit_bytes=2**20),
        )(pieces)

    with jax.named_scope("left"):
        left, gradient, feedback = pl.pallas_call(
            left_kernel,
            out_shape=(jax.ShapeDtypeStruct((wide // LANES,) + tile, F32), held, held),
            in_specs=[hbm, hbm, hbm],
            out_specs=[vmem, vmem, vmem],
            scratch_shapes=[pltpu.VMEM((RANK, units), F32), pltpu.SemaphoreType.DMA((3, steps))],
            compiler_params=params,
        )(*(pltpu.with_memory_space_constraint(x, pltpu.HBM) for x in (right_prior.T, gradient, feedback)))
    with jax.named_scope("left_sum"):
        pieces = spread(lax.all_to_all(left, "tensor", 0, 0), replicas)
        pieces = spread(lax.all_to_all(pieces, "dp", 0, 0), parts)
        left = lax.all_to_all(pieces, "tensor", 0, 0)
    with jax.named_scope("right"):
        basis, right = pl.pallas_call(
            right_kernel,
            out_shape=(jax.ShapeDtypeStruct((3 * RANK, wide), F32), jax.ShapeDtypeStruct((replicas, RANK, units), F32)),
            in_specs=[vmem, vmem, vmem],
            out_specs=[vmem, vmem],
            compiler_params=params,
        )(left, gradient, feedback)
    with jax.named_scope("right_sum"):
        rights = lax.all_to_all(right, "dp", 0, 0)
    with jax.named_scope("rebuild"):
        update, residue, right_next = pl.pallas_call(
            functools.partial(rebuild_kernel, replicas),
            out_shape=(
                jax.ShapeDtypeStruct((units, CHUNK), BF16),
                jax.ShapeDtypeStruct((units, wide), BF16),
                jax.ShapeDtypeStruct((RANK, units), F32),
            ),
            in_specs=[vmem, vmem, vmem, vmem],
            out_specs=[hbm, hbm, vmem],
            scratch_shapes=[
                pltpu.VMEM((units, wide), BF16),
                pltpu.VMEM((units, CHUNK), BF16),
                pltpu.SemaphoreType.DMA((steps + 1,)),
            ],
            compiler_params=params,
        )(rights, basis, gradient, feedback)
    return update.T, residue.T[None], right_next.T


def solution(mesh):
    placed = (P("dp", None, "tensor"), P("dp", None, "tensor"), P("tensor", None))
    return jax.shard_map(
        shards,
        mesh=mesh,
        in_specs=placed,
        out_specs=(P("dp", "tensor"), P("dp", None, "tensor"), P("tensor", None)),
        check_vma=False,
    )
```

```python
import functools

import jax
import jax.numpy as jnp
from jax import lax
from jax.experimental import pallas as pl
from jax.experimental.pallas import tpu as pltpu
from jax.sharding import PartitionSpec as P

RANK = 8
LANES = 128
CHUNK = 512
F32 = jnp.float32
BF16 = jnp.bfloat16
LAST_BOTH = (((1,), (1,)), ((), ()))
FIRST_BOTH = (((0,), (0,)), ((), ()))


def thirds(x):
    high = x.astype(BF16).astype(F32)
    rest = x - high
    middle = rest.astype(BF16).astype(F32)
    low = (rest - middle).astype(BF16).astype(F32)
    return high, middle, low


def folded(total):
    return total[:RANK] + total[RANK : 2 * RANK] + total[2 * RANK :]


def left_kernel(prior_far, gradient_far, feedback_far, left, gradient, feedback, prior, sems):
    steps = gradient.shape[1] // CHUNK
    prior_copy = pltpu.make_async_copy(prior_far, prior, sems.at[2, 0])
    prior_copy.start()
    for step in range(steps):
        columns = pl.ds(step * CHUNK, CHUNK)
        for which, (source, target) in enumerate(((gradient_far, gradient), (feedback_far, feedback))):
            copy = pltpu.make_async_copy(source.at[:, columns], target.at[:, columns], sems.at[which, step])
            copy.start()
    prior_copy.wait()
    terms = jnp.concatenate(thirds(prior[...]), axis=0).astype(BF16)

    @pl.loop(0, steps)
    def _(step):
        columns = pl.ds(pl.multiple_of(step * CHUNK, CHUNK), CHUNK)
        for which, (source, target) in enumerate(((gradient_far, gradient), (feedback_far, feedback))):
            pltpu.make_async_copy(source.at[:, columns], target.at[:, columns], sems.at[which, step]).wait()
        total = jnp.dot(terms, gradient[:, columns], preferred_element_type=F32)
        total += jnp.dot(terms, feedback[:, columns], preferred_element_type=F32)
        total = folded(total)
        for tile in range(CHUNK // LANES):
            left[step * (CHUNK // LANES) + tile] = total[:, tile * LANES : (tile + 1) * LANES]


def spread_kernel(pieces, copies):
    total = pieces[0]
    for piece in range(1, pieces.shape[0]):
        total = total + pieces[piece]
    for copy in range(copies.shape[0]):
        copies[copy] = total


def put_thirds(tiles, where):
    for tile in range(tiles.shape[0]):
        for third, part in enumerate(thirds(tiles[tile])):
            where[third * RANK : (third + 1) * RANK, tile * LANES : (tile + 1) * LANES] = part


def right_kernel(left, gradient, feedback, basis, right, left_terms):
    put_thirds(left[...], left_terms)
    terms = left_terms[...].astype(BF16)
    product = lax.dot_general(terms, gradient[...], LAST_BOTH, preferred_element_type=F32)
    product += lax.dot_general(terms, feedback[...], LAST_BOTH, preferred_element_type=F32)
    product = folded(product)
    value = left[...]
    rank_row = lax.broadcasted_iota(jnp.int32, (RANK, 1), 0)
    scale = jnp.zeros((RANK, 1), F32)
    tile = (RANK, LANES)
    change = (lax.broadcasted_iota(jnp.int32, tile, 0) == lax.broadcasted_iota(jnp.int32, tile, 1)).astype(F32)
    for column in range(RANK):
        row = value[:, column : column + 1, :]
        products = value * row
        count = products.shape[0]
        while count > 1:
            count //= 2
            products = products[:count] + products[count : 2 * count]
        inner = jnp.sum(products[0], axis=1, keepdims=True)
        inverse = lax.rsqrt(inner[column : column + 1] + 1e-06)
        scale = jnp.where(rank_row == column, inverse, scale)
        if column < RANK - 1:
            factor = jnp.where(rank_row > column, inner * inverse * inverse, 0.0)
            value = value - factor[None] * row
            change = change - factor * change[column : column + 1]
    put_thirds(value * scale[None], basis)
    change = change * scale
    total = change[:, 0:1] * product[0:1]
    for column in range(1, RANK):
        total = total + change[:, column : column + 1] * product[column : column + 1]
    for copy in range(right.shape[0]):
        right[copy] = total


def rebuild_kernel(
    replicas, rights, basis, gradient, feedback, update, residue, right_next, staged, slab, right, sems
):
    mine = lax.axis_index("dp")
    wide = gradient.shape[1]
    steps = wide // CHUNK
    total = rights[0]
    for replica in range(1, replicas):
        total = total + rights[replica]
    total = total * (1.0 / replicas)
    right[...] = total
    copies = [pltpu.make_async_copy(right, right_next, sems.at[steps + 1])]
    copies[0].start()
    first, second, third = thirds(total)
    lhs = jnp.concatenate((first, first, first, second, second, third), axis=0).astype(BF16)

    def rebuilt(columns):
        one, two, three = (basis[RANK * k : RANK * (k + 1), columns] for k in range(3))
        rhs = jnp.concatenate((one, two, three, one, two, one), axis=0).astype(BF16)
        return lax.dot_general(lhs, rhs, FIRST_BOTH, preferred_element_type=F32)

    for step in range(steps):
        columns = pl.ds(step * CHUNK, CHUNK)
        corrected = gradient[:, columns].astype(F32) + feedback[:, columns].astype(F32)
        staged[:, columns] = (corrected - rebuilt(columns)).astype(BF16)
        copy = pltpu.make_async_copy(staged.at[:, columns], residue.at[:, columns], sems.at[step])
        copy.start()
        copies.append(copy)
        if step == 0:
            slab[...] = rebuilt(pl.ds(pl.multiple_of(mine * CHUNK, CHUNK), CHUNK)).astype(BF16)
            copy = pltpu.make_async_copy(slab, update, sems.at[steps])
            copy.start()
            copies.append(copy)
    for copy in copies:
        copy.wait()


def shards(gradient, feedback, right_prior):
    gradient, feedback = gradient[0].T, feedback[0].T
    units, wide = gradient.shape
    replicas, parts = lax.axis_size("dp"), lax.axis_size("tensor")
    steps = wide // CHUNK
    vmem = pl.BlockSpec(memory_space=pltpu.VMEM)
    hbm = pl.BlockSpec(memory_space=pltpu.HBM)
    held = pltpu.VMEM((units, wide), BF16)
    params = pltpu.CompilerParams(vmem_limit_bytes=16 * 2**20)
    tile = (RANK, LANES)

    def spread(pieces, count):
        return pl.pallas_call(
            spread_kernel,
            out_shape=jax.ShapeDtypeStruct((count,) + tile, F32),
            in_specs=[vmem],
            out_specs=vmem,
            compiler_params=pltpu.CompilerParams(vmem_limit_bytes=2**20),
        )(pieces)

    with jax.named_scope("left"):
        left, gradient, feedback = pl.pallas_call(
            left_kernel,
            out_shape=(jax.ShapeDtypeStruct((wide // LANES,) + tile, F32), held, held),
            in_specs=[hbm, hbm, hbm],
            out_specs=[vmem] * 3,
            scratch_shapes=[pltpu.VMEM((RANK, units), F32), pltpu.SemaphoreType.DMA((3, steps))],
            compiler_params=params,
        )(*(pltpu.with_memory_space_constraint(x, pltpu.HBM) for x in (right_prior.T, gradient, feedback)))
    with jax.named_scope("left_sum"):
        pieces = spread(lax.all_to_all(left, "tensor", 0, 0), replicas)
        pieces = spread(lax.all_to_all(pieces, "dp", 0, 0), parts)
        left = lax.all_to_all(pieces, "tensor", 0, 0)
    with jax.named_scope("right"):
        basis, right = pl.pallas_call(
            right_kernel,
            out_shape=(jax.ShapeDtypeStruct((3 * RANK, wide), F32), jax.ShapeDtypeStruct((replicas, RANK, units), F32)),
            in_specs=[vmem, vmem, vmem],
            out_specs=[vmem, vmem],
            scratch_shapes=[pltpu.VMEM((3 * RANK, wide), F32)],
            compiler_params=params,
        )(left, gradient, feedback)
    with jax.named_scope("right_sum"):
        rights = lax.all_to_all(right, "dp", 0, 0)
    with jax.named_scope("rebuild"):
        update, residue, right_next = pl.pallas_call(
            functools.partial(rebuild_kernel, replicas),
            out_shape=(
                jax.ShapeDtypeStruct((units, CHUNK), BF16),
                jax.ShapeDtypeStruct((units, wide), BF16),
                jax.ShapeDtypeStruct((RANK, units), F32),
            ),
            in_specs=[vmem] * 4,
            out_specs=[hbm] * 3,
            scratch_shapes=[
                pltpu.VMEM((units, wide), BF16),
                pltpu.VMEM((units, CHUNK), BF16),
                pltpu.VMEM((RANK, units), F32),
                pltpu.SemaphoreType.DMA((steps + 2,)),
            ],
            compiler_params=params,
        )(rights, basis, gradient, feedback)
    return update.T, residue.T[None], right_next.T


def solution(mesh):
    placed = (P("dp", None, "tensor"), P("dp", None, "tensor"), P("tensor", None))
    return jax.shard_map(
        shards,
        mesh=mesh,
        in_specs=placed,
        out_specs=(P("dp", "tensor"), P("dp", None, "tensor"), P("tensor", None)),
        check_vma=False,
    )
```

```python
import functools

import jax
import jax.numpy as jnp
from jax import lax
from jax.experimental import pallas as pl
from jax.experimental.pallas import tpu as pltpu
from jax.sharding import PartitionSpec as P

RANK = 8
LANES = 128
CHUNK = 512
SIDE = 4
CORES = 2
F32 = jnp.float32
BF16 = jnp.bfloat16
LAST_BOTH = (((1,), (1,)), ((), ()))
FIRST_BOTH = (((0,), (0,)), ((), ()))


def thirds(x):
    high = x.astype(BF16).astype(F32)
    rest = x - high
    middle = rest.astype(BF16).astype(F32)
    low = (rest - middle).astype(BF16).astype(F32)
    return high, middle, low


def folded(total):
    return total[:RANK] + total[RANK : 2 * RANK] + total[2 * RANK :]


def left_kernel(prior_far, gradient_far, feedback_far, left, gradient, feedback, prior, sems):
    steps = gradient.shape[1] // CHUNK
    prior_copy = pltpu.make_async_copy(prior_far, prior, sems.at[2, 0])
    prior_copy.start()
    for step in range(steps):
        columns = pl.ds(step * CHUNK, CHUNK)
        for which, (source, target) in enumerate(((gradient_far, gradient), (feedback_far, feedback))):
            copy = pltpu.make_async_copy(source.at[:, columns], target.at[:, columns], sems.at[which, step])
            copy.start()
    prior_copy.wait()
    terms = jnp.concatenate(thirds(prior[...]), axis=0).astype(BF16)

    @pl.loop(0, steps)
    def _(step):
        columns = pl.ds(pl.multiple_of(step * CHUNK, CHUNK), CHUNK)
        for which, (source, target) in enumerate(((gradient_far, gradient), (feedback_far, feedback))):
            pltpu.make_async_copy(source.at[:, columns], target.at[:, columns], sems.at[which, step]).wait()
        total = jnp.dot(terms, gradient[:, columns], preferred_element_type=F32)
        total += jnp.dot(terms, feedback[:, columns], preferred_element_type=F32)
        total = folded(total)
        for tile in range(CHUNK // LANES):
            left[step * (CHUNK // LANES) + tile] = total[:, tile * LANES : (tile + 1) * LANES]


def spread_kernel(pieces, copies):
    total = pieces[0]
    for piece in range(1, pieces.shape[0]):
        total = total + pieces[piece]
    for copy in range(copies.shape[0]):
        copies[copy] = total


def right_kernel(left, gradient, feedback, basis, right):
    block = CHUNK // LANES
    product = jnp.zeros((3 * RANK, gradient.shape[0]), F32)
    for step in range(gradient.shape[1] // CHUNK):
        columns = pl.ds(step * CHUNK, CHUNK)
        rows = jnp.concatenate([left[step * block + tile] for tile in range(block)], axis=1)
        terms = jnp.concatenate(thirds(rows), axis=0).astype(BF16)
        product += lax.dot_general(terms, gradient[:, columns], LAST_BOTH, preferred_element_type=F32)
        product += lax.dot_general(terms, feedback[:, columns], LAST_BOTH, preferred_element_type=F32)
    product = folded(product)
    value = left[...]
    rank_row = lax.broadcasted_iota(jnp.int32, (RANK, 1), 0)
    scale = jnp.zeros((RANK, 1), F32)
    tile = (RANK, LANES)
    change = (lax.broadcasted_iota(jnp.int32, tile, 0) == lax.broadcasted_iota(jnp.int32, tile, 1)).astype(F32)
    for column in range(RANK):
        row = value[:, column : column + 1, :]
        products = value * row
        count = products.shape[0]
        while count > 1:
            count //= 2
            products = products[:count] + products[count : 2 * count]
        inner = jnp.sum(products[0], axis=1, keepdims=True)
        inverse = lax.rsqrt(inner[column : column + 1] + 1e-06)
        scale = jnp.where(rank_row == column, inverse, scale)
        if column < RANK - 1:
            factor = jnp.where(rank_row > column, inner * inverse * inverse, 0.0)
            value = value - factor[None] * row
            change = change - factor * change[column : column + 1]
    value = value * scale[None]
    for tile in range(value.shape[0]):
        one, two, three = thirds(value[tile])
        rows = jnp.concatenate((one, two, three, one, two, one), axis=0)
        basis[:, tile * LANES : (tile + 1) * LANES] = rows.astype(BF16)
    change = change * scale
    total = change[:, 0:1] * product[0:1]
    for column in range(1, RANK):
        total = total + change[:, column : column + 1] * product[column : column + 1]
    for copy in range(right.shape[0]):
        right[copy] = total


def rebuild_kernel(
    replicas, rights, basis, gradient, feedback, update, residue, right_next, staged, slab, right, sems
):
    mine = lax.axis_index("dp")
    wide = gradient.shape[1]
    steps = wide // CHUNK
    total = rights[0]
    for replica in range(1, replicas):
        total = total + rights[replica]
    total = total * (1.0 / replicas)
    right[...] = total
    copies = [pltpu.make_async_copy(right, right_next, sems.at[steps + 1])]
    copies[0].start()
    first, second, third = thirds(total)
    lhs = jnp.concatenate((first, first, first, second, second, third), axis=0).astype(BF16)

    def rebuilt(columns):
        return lax.dot_general(lhs, basis[:, columns], FIRST_BOTH, preferred_element_type=F32)

    for step in range(steps):
        columns = pl.ds(step * CHUNK, CHUNK)
        corrected = gradient[:, columns].astype(F32) + feedback[:, columns].astype(F32)
        staged[:, columns] = (corrected - rebuilt(columns)).astype(BF16)
        copy = pltpu.make_async_copy(staged.at[:, columns], residue.at[:, columns], sems.at[step])
        copy.start()
        copies.append(copy)
        if step == 0:
            slab[...] = rebuilt(pl.ds(pl.multiple_of(mine * CHUNK, CHUNK), CHUNK)).astype(BF16)
            copy = pltpu.make_async_copy(slab, update, sems.at[steps])
            copy.start()
            copies.append(copy)
    for copy in copies:
        copy.wait()


def plane_groups(replicas):
    halves = [
        [(y * SIDE + x) * CORES + core for x in pair for y in range(SIDE) for core in range(CORES)]
        for pair in ((0, 1), (3, 2))
    ]
    parts = SIDE * SIDE * CORES
    mixed = [[replica * parts + place for replica in range(replicas) for place in pair] for pair in zip(*halves)]
    return halves, mixed


def shards(gradient, feedback, right_prior):
    gradient, feedback = gradient[0].T, feedback[0].T
    units, wide = gradient.shape
    replicas, parts = lax.axis_size("dp"), lax.axis_size("tensor")
    steps = wide // CHUNK
    vmem = pl.BlockSpec(memory_space=pltpu.VMEM)
    hbm = pl.BlockSpec(memory_space=pltpu.HBM)
    held = pltpu.VMEM((units, wide), BF16)
    params = pltpu.CompilerParams(vmem_limit_bytes=16 * 2**20)
    tile = (RANK, LANES)

    def spread(pieces, count):
        return pl.pallas_call(
            spread_kernel,
            out_shape=jax.ShapeDtypeStruct((count,) + pieces.shape[1:], F32),
            in_specs=[vmem],
            out_specs=vmem,
            compiler_params=pltpu.CompilerParams(vmem_limit_bytes=2**20),
        )(pieces)

    with jax.named_scope("left"):
        left, gradient, feedback = pl.pallas_call(
            left_kernel,
            out_shape=(jax.ShapeDtypeStruct((wide // LANES,) + tile, F32), held, held),
            in_specs=[hbm, hbm, hbm],
            out_specs=[vmem] * 3,
            scratch_shapes=[pltpu.VMEM((RANK, units), F32), pltpu.SemaphoreType.DMA((3, steps))],
            compiler_params=params,
        )(*(pltpu.with_memory_space_constraint(x, pltpu.HBM) for x in (right_prior.T, gradient, feedback)))
    halves, mixed = plane_groups(replicas)
    members, reducers = len(halves[0]), len(mixed[0])
    share = (wide // LANES // members,) + tile
    with jax.named_scope("left_sum"):
        pieces = left.reshape((members,) + share)
        pieces = spread(lax.all_to_all(pieces, "tensor", 0, 0, axis_index_groups=halves), reducers)
        pieces = spread(lax.all_to_all(pieces, ("dp", "tensor"), 0, 0, axis_index_groups=mixed), members)
        left = lax.all_to_all(pieces, "tensor", 0, 0, axis_index_groups=halves)
        left = left.reshape((wide // LANES,) + tile)
    with jax.named_scope("right"):
        basis, right = pl.pallas_call(
            right_kernel,
            out_shape=(jax.ShapeDtypeStruct((6 * RANK, wide), BF16), jax.ShapeDtypeStruct((replicas, RANK, units), F32)),
            in_specs=[vmem, vmem, vmem],
            out_specs=[vmem, vmem],
            compiler_params=params,
        )(left, gradient, feedback)
    with jax.named_scope("right_sum"):
        rights = lax.all_to_all(right, "dp", 0, 0)
    with jax.named_scope("rebuild"):
        update, residue, right_next = pl.pallas_call(
            functools.partial(rebuild_kernel, replicas),
            out_shape=(
                jax.ShapeDtypeStruct((units, CHUNK), BF16),
                jax.ShapeDtypeStruct((units, wide), BF16),
                jax.ShapeDtypeStruct((RANK, units), F32),
            ),
            in_specs=[vmem] * 4,
            out_specs=[hbm] * 3,
            scratch_shapes=[
                pltpu.VMEM((units, wide), BF16),
                pltpu.VMEM((units, CHUNK), BF16),
                pltpu.VMEM((RANK, units), F32),
                pltpu.SemaphoreType.DMA((steps + 2,)),
            ],
            compiler_params=params,
        )(rights, basis, gradient, feedback)
    return update.T, residue.T[None], right_next.T


def solution(mesh):
    placed = (P("dp", None, "tensor"), P("dp", None, "tensor"), P("tensor", None))
    return jax.shard_map(
        shards,
        mesh=mesh,
        in_specs=placed,
        out_specs=(P("dp", "tensor"), P("dp", None, "tensor"), P("tensor", None)),
        check_vma=False,
    )
```

```python
import functools

import jax
import jax.numpy as jnp
from jax import lax
from jax.experimental import pallas as pl
from jax.experimental.pallas import tpu as pltpu
from jax.sharding import PartitionSpec as P

RANK = 8
LANES = 128
CHUNK = 512
SIDE = 4
CORES = 2
DP_ORDER = [0, 4, 2, 6, 1, 5, 3, 7]
F32 = jnp.float32
BF16 = jnp.bfloat16
LAST_BOTH = (((1,), (1,)), ((), ()))
FIRST_BOTH = (((0,), (0,)), ((), ()))


def thirds(x):
    high = x.astype(BF16).astype(F32)
    rest = x - high
    middle = rest.astype(BF16).astype(F32)
    low = (rest - middle).astype(BF16).astype(F32)
    return high, middle, low


def folded(total):
    return total[:RANK] + total[RANK : 2 * RANK] + total[2 * RANK :]


def left_kernel(prior_far, gradient_far, feedback_far, left, gradient, feedback, prior, sems):
    steps = gradient.shape[1] // CHUNK
    prior_copy = pltpu.make_async_copy(prior_far, prior, sems.at[2, 0])
    prior_copy.start()
    for step in range(steps):
        columns = pl.ds(step * CHUNK, CHUNK)
        for which, (source, target) in enumerate(((gradient_far, gradient), (feedback_far, feedback))):
            copy = pltpu.make_async_copy(source.at[:, columns], target.at[:, columns], sems.at[which, step])
            copy.start()
    prior_copy.wait()
    terms = jnp.concatenate(thirds(prior[...]), axis=0).astype(BF16)

    @pl.loop(0, steps)
    def _(step):
        columns = pl.ds(pl.multiple_of(step * CHUNK, CHUNK), CHUNK)
        for which, (source, target) in enumerate(((gradient_far, gradient), (feedback_far, feedback))):
            pltpu.make_async_copy(source.at[:, columns], target.at[:, columns], sems.at[which, step]).wait()
        total = jnp.dot(terms, gradient[:, columns], preferred_element_type=F32)
        total += jnp.dot(terms, feedback[:, columns], preferred_element_type=F32)
        total = folded(total)
        for tile in range(CHUNK // LANES):
            left[step * (CHUNK // LANES) + tile] = total[:, tile * LANES : (tile + 1) * LANES]


def spread_kernel(pieces, copies):
    total = pieces[0]
    for piece in range(1, pieces.shape[0]):
        total = total + pieces[piece]
    for copy in range(copies.shape[0]):
        copies[copy] = total


def right_kernel(left, gradient, feedback, basis, right):
    block = CHUNK // LANES
    product = jnp.zeros((3 * RANK, gradient.shape[0]), F32)
    for step in range(gradient.shape[1] // CHUNK):
        columns = pl.ds(step * CHUNK, CHUNK)
        rows = jnp.concatenate([left[step * block + tile] for tile in range(block)], axis=1)
        terms = jnp.concatenate(thirds(rows), axis=0).astype(BF16)
        product += lax.dot_general(terms, gradient[:, columns], LAST_BOTH, preferred_element_type=F32)
        product += lax.dot_general(terms, feedback[:, columns], LAST_BOTH, preferred_element_type=F32)
    product = folded(product)
    value = left[...]
    rank_row = lax.broadcasted_iota(jnp.int32, (RANK, 1), 0)
    scale = jnp.zeros((RANK, 1), F32)
    tile = (RANK, LANES)
    change = (lax.broadcasted_iota(jnp.int32, tile, 0) == lax.broadcasted_iota(jnp.int32, tile, 1)).astype(F32)
    for column in range(RANK):
        row = value[:, column : column + 1, :]
        products = value * row
        count = products.shape[0]
        while count > 1:
            count //= 2
            products = products[:count] + products[count : 2 * count]
        inner = jnp.sum(products[0], axis=1, keepdims=True)
        inverse = lax.rsqrt(inner[column : column + 1] + 1e-06)
        scale = jnp.where(rank_row == column, inverse, scale)
        if column < RANK - 1:
            factor = jnp.where(rank_row > column, inner * inverse * inverse, 0.0)
            value = value - factor[None] * row
            change = change - factor * change[column : column + 1]
    value = value * scale[None]
    for tile in range(value.shape[0]):
        one, two, three = thirds(value[tile])
        rows = jnp.concatenate((one, two, three, one, two, one), axis=0)
        basis[:, tile * LANES : (tile + 1) * LANES] = rows.astype(BF16)
    change = change * scale
    total = change[:, 0:1] * product[0:1]
    for column in range(1, RANK):
        total = total + change[:, column : column + 1] * product[column : column + 1]
    for copy in range(right.shape[0]):
        right[copy] = total


def rebuild_kernel(
    replicas, rights, basis, gradient, feedback, update, residue, right_next, staged, slab, right, sems
):
    mine = lax.axis_index("dp")
    wide = gradient.shape[1]
    steps = wide // CHUNK
    total = rights[0]
    for replica in range(1, replicas):
        total = total + rights[replica]
    total = total * (1.0 / replicas)
    right[...] = total
    copies = [pltpu.make_async_copy(right, right_next, sems.at[steps + 1])]
    copies[0].start()
    first, second, third = thirds(total)
    lhs = jnp.concatenate((first, first, first, second, second, third), axis=0).astype(BF16)

    def rebuilt(columns):
        return lax.dot_general(lhs, basis[:, columns], FIRST_BOTH, preferred_element_type=F32)

    for step in range(steps):
        columns = pl.ds(step * CHUNK, CHUNK)
        corrected = gradient[:, columns].astype(F32) + feedback[:, columns].astype(F32)
        staged[:, columns] = (corrected - rebuilt(columns)).astype(BF16)
        copy = pltpu.make_async_copy(staged.at[:, columns], residue.at[:, columns], sems.at[step])
        copy.start()
        copies.append(copy)
        if step == 0:
            slab[...] = rebuilt(pl.ds(pl.multiple_of(mine * CHUNK, CHUNK), CHUNK)).astype(BF16)
            copy = pltpu.make_async_copy(slab, update, sems.at[steps])
            copy.start()
            copies.append(copy)
    for copy in copies:
        copy.wait()


def plane_groups(replicas):
    halves = [
        [(y * SIDE + x) * CORES + core for core in range(CORES) for y in range(SIDE) for x in pair]
        for pair in ((0, 1), (3, 2))
    ]
    parts = SIDE * SIDE * CORES
    mixed = [[replica * parts + place for place in pair for replica in reversed(range(replicas))] for pair in zip(*halves)]
    return halves, mixed


def shards(gradient, feedback, right_prior):
    gradient, feedback = gradient[0].T, feedback[0].T
    units, wide = gradient.shape
    replicas, parts = lax.axis_size("dp"), lax.axis_size("tensor")
    steps = wide // CHUNK
    vmem = pl.BlockSpec(memory_space=pltpu.VMEM)
    hbm = pl.BlockSpec(memory_space=pltpu.HBM)
    held = pltpu.VMEM((units, wide), BF16)
    params = pltpu.CompilerParams(vmem_limit_bytes=16 * 2**20)
    tile = (RANK, LANES)

    def spread(pieces, count):
        return pl.pallas_call(
            spread_kernel,
            out_shape=jax.ShapeDtypeStruct((count,) + pieces.shape[1:], F32),
            in_specs=[vmem],
            out_specs=vmem,
            compiler_params=pltpu.CompilerParams(vmem_limit_bytes=2**20),
        )(pieces)

    with jax.named_scope("left"):
        left, gradient, feedback = pl.pallas_call(
            left_kernel,
            out_shape=(jax.ShapeDtypeStruct((wide // LANES,) + tile, F32), held, held),
            in_specs=[hbm, hbm, hbm],
            out_specs=[vmem] * 3,
            scratch_shapes=[pltpu.VMEM((RANK, units), F32), pltpu.SemaphoreType.DMA((3, steps))],
            compiler_params=params,
        )(*(pltpu.with_memory_space_constraint(x, pltpu.HBM) for x in (right_prior.T, gradient, feedback)))
    halves, mixed = plane_groups(replicas)
    members, reducers = len(halves[0]), len(mixed[0])
    share = (wide // LANES // members,) + tile
    with jax.named_scope("left_sum"):
        pieces = left.reshape((members,) + share)
        pieces = spread(lax.all_to_all(pieces, "tensor", 0, 0, axis_index_groups=halves), reducers)
        pieces = spread(lax.all_to_all(pieces, ("dp", "tensor"), 0, 0, axis_index_groups=mixed), members)
        left = lax.all_to_all(pieces, "tensor", 0, 0, axis_index_groups=halves)
        left = left.reshape((wide // LANES,) + tile)
    with jax.named_scope("right"):
        basis, right = pl.pallas_call(
            right_kernel,
            out_shape=(jax.ShapeDtypeStruct((6 * RANK, wide), BF16), jax.ShapeDtypeStruct((replicas, RANK, units), F32)),
            in_specs=[vmem, vmem, vmem],
            out_specs=[vmem, vmem],
            compiler_params=params,
        )(left, gradient, feedback)
    with jax.named_scope("right_sum"):
        rights = lax.all_to_all(right, "dp", 0, 0, axis_index_groups=[DP_ORDER])
    with jax.named_scope("rebuild"):
        update, residue, right_next = pl.pallas_call(
            functools.partial(rebuild_kernel, replicas),
            out_shape=(
                jax.ShapeDtypeStruct((units, CHUNK), BF16),
                jax.ShapeDtypeStruct((units, wide), BF16),
                jax.ShapeDtypeStruct((RANK, units), F32),
            ),
            in_specs=[vmem] * 4,
            out_specs=[hbm] * 3,
            scratch_shapes=[
                pltpu.VMEM((units, wide), BF16),
                pltpu.VMEM((units, CHUNK), BF16),
                pltpu.VMEM((RANK, units), F32),
                pltpu.SemaphoreType.DMA((steps + 2,)),
            ],
            compiler_params=params,
        )(rights, basis, gradient, feedback)
    return update.T, residue.T[None], right_next.T


def solution(mesh):
    placed = (P("dp", None, "tensor"), P("dp", None, "tensor"), P("tensor", None))
    return jax.shard_map(
        shards,
        mesh=mesh,
        in_specs=placed,
        out_specs=(P("dp", "tensor"), P("dp", None, "tensor"), P("tensor", None)),
        check_vma=False,
    )
```

```python
import functools

import jax
import jax.numpy as jnp
from jax import lax
from jax.experimental import pallas as pl
from jax.experimental.pallas import tpu as pltpu
from jax.sharding import PartitionSpec as P

RANK = 8
LANES = 128
CHUNK = 512
SIDE = 4
CORES = 2
DP_ORDER = [0, 4, 2, 6, 1, 5, 3, 7]
F32 = jnp.float32
BF16 = jnp.bfloat16
LAST_BOTH = (((1,), (1,)), ((), ()))
FIRST_BOTH = (((0,), (0,)), ((), ()))


def thirds(x):
    high = x.astype(BF16).astype(F32)
    rest = x - high
    middle = rest.astype(BF16).astype(F32)
    low = (rest - middle).astype(BF16).astype(F32)
    return high, middle, low


def folded(total):
    return total[:RANK] + total[RANK : 2 * RANK] + total[2 * RANK :]


def left_kernel(prior_far, gradient_far, feedback_far, left, gradient, feedback, prior, sems):
    steps = gradient.shape[1] // CHUNK
    prior_copy = pltpu.make_async_copy(prior_far, prior, sems.at[2, 0])
    prior_copy.start()
    for step in range(steps):
        columns = pl.ds(step * CHUNK, CHUNK)
        for which, (source, target) in enumerate(((gradient_far, gradient), (feedback_far, feedback))):
            copy = pltpu.make_async_copy(source.at[:, columns], target.at[:, columns], sems.at[which, step])
            copy.start()
    prior_copy.wait()
    terms = jnp.concatenate(thirds(prior[...]), axis=0).astype(BF16)

    @pl.loop(0, steps)
    def _(step):
        columns = pl.ds(pl.multiple_of(step * CHUNK, CHUNK), CHUNK)
        for which, (source, target) in enumerate(((gradient_far, gradient), (feedback_far, feedback))):
            pltpu.make_async_copy(source.at[:, columns], target.at[:, columns], sems.at[which, step]).wait()
        total = jnp.dot(terms, gradient[:, columns], preferred_element_type=F32)
        total += jnp.dot(terms, feedback[:, columns], preferred_element_type=F32)
        total = folded(total)
        for tile in range(CHUNK // LANES):
            left[step * (CHUNK // LANES) + tile] = total[:, tile * LANES : (tile + 1) * LANES]


def spread_kernel(pieces, copies):
    total = pieces[0]
    for piece in range(1, pieces.shape[0]):
        total = total + pieces[piece]
    for copy in range(copies.shape[0]):
        copies[copy] = total


def right_kernel(left, gradient, feedback, basis, right):
    block = CHUNK // LANES
    product = jnp.zeros((3 * RANK, gradient.shape[0]), F32)
    for step in range(gradient.shape[1] // CHUNK):
        columns = pl.ds(step * CHUNK, CHUNK)
        rows = jnp.concatenate([left[step * block + tile] for tile in range(block)], axis=1)
        terms = jnp.concatenate(thirds(rows), axis=0).astype(BF16)
        product += lax.dot_general(terms, gradient[:, columns], LAST_BOTH, preferred_element_type=F32)
        product += lax.dot_general(terms, feedback[:, columns], LAST_BOTH, preferred_element_type=F32)
    product = folded(product)
    value = left[...]
    rank_row = lax.broadcasted_iota(jnp.int32, (RANK, 1), 0)
    scale = jnp.zeros((RANK, 1), F32)
    tile = (RANK, LANES)
    change = (lax.broadcasted_iota(jnp.int32, tile, 0) == lax.broadcasted_iota(jnp.int32, tile, 1)).astype(F32)
    for column in range(RANK):
        row = value[:, column : column + 1, :]
        products = value * row
        count = products.shape[0]
        while count > 1:
            count //= 2
            products = products[:count] + products[count : 2 * count]
        inner = jnp.sum(products[0], axis=1, keepdims=True)
        inverse = lax.rsqrt(inner[column : column + 1] + 1e-06)
        scale = jnp.where(rank_row == column, inverse, scale)
        if column < RANK - 1:
            factor = jnp.where(rank_row > column, inner * inverse * inverse, 0.0)
            value = value - factor[None] * row
            change = change - factor * change[column : column + 1]
    value = value * scale[None]
    for tile in range(value.shape[0]):
        one, two, three = thirds(value[tile])
        rows = jnp.concatenate((one, two, three, one, two, one), axis=0)
        basis[:, tile * LANES : (tile + 1) * LANES] = rows.astype(BF16)
    change = change * scale
    total = change[:, 0:1] * product[0:1]
    for column in range(1, RANK):
        total = total + change[:, column : column + 1] * product[column : column + 1]
    for copy in range(right.shape[0]):
        right[copy] = total


def rebuild_kernel(
    replicas, rights, basis, gradient, feedback, update, residue, right_next, staged, slab, right, sems
):
    mine = lax.axis_index("dp")
    wide = gradient.shape[1]
    steps = wide // CHUNK
    total = rights[0]
    for replica in range(1, replicas):
        total = total + rights[replica]
    total = total * (1.0 / replicas)
    right[...] = total
    copies = [pltpu.make_async_copy(right, right_next, sems.at[steps + 1])]
    copies[0].start()
    first, second, third = thirds(total)
    lhs = jnp.concatenate((first, first, first, second, second, third), axis=0).astype(BF16)

    def rebuilt(columns):
        return lax.dot_general(lhs, basis[:, columns], FIRST_BOTH, preferred_element_type=F32)

    for step in range(steps):
        columns = pl.ds(step * CHUNK, CHUNK)
        corrected = gradient[:, columns].astype(F32) + feedback[:, columns].astype(F32)
        staged[:, columns] = (corrected - rebuilt(columns)).astype(BF16)
        copy = pltpu.make_async_copy(staged.at[:, columns], residue.at[:, columns], sems.at[step])
        copy.start()
        copies.append(copy)
        if step == 0:
            slab[...] = rebuilt(pl.ds(pl.multiple_of(mine * CHUNK, CHUNK), CHUNK)).astype(BF16)
            copy = pltpu.make_async_copy(slab, update, sems.at[steps])
            copy.start()
            copies.append(copy)
    for copy in copies:
        copy.wait()


def plane_groups(replicas):
    halves = [
        [(y * SIDE + x) * CORES + core for core in reversed(range(CORES)) for y in reversed(range(SIDE)) for x in pair]
        for pair in ((0, 1), (3, 2))
    ]
    parts = SIDE * SIDE * CORES
    mixed = [[replica * parts + place for place in reversed(pair) for replica in reversed(range(replicas))] for pair in zip(*halves)]
    return halves, mixed


def shards(gradient, feedback, right_prior):
    gradient, feedback = gradient[0].T, feedback[0].T
    units, wide = gradient.shape
    replicas, parts = lax.axis_size("dp"), lax.axis_size("tensor")
    steps = wide // CHUNK
    vmem = pl.BlockSpec(memory_space=pltpu.VMEM)
    hbm = pl.BlockSpec(memory_space=pltpu.HBM)
    held = pltpu.VMEM((units, wide), BF16)
    params = pltpu.CompilerParams(vmem_limit_bytes=16 * 2**20)
    tile = (RANK, LANES)

    def spread(pieces, count):
        return pl.pallas_call(
            spread_kernel,
            out_shape=jax.ShapeDtypeStruct((count,) + pieces.shape[1:], F32),
            in_specs=[vmem],
            out_specs=vmem,
            compiler_params=pltpu.CompilerParams(vmem_limit_bytes=2**20),
        )(pieces)

    with jax.named_scope("left"):
        left, gradient, feedback = pl.pallas_call(
            left_kernel,
            out_shape=(jax.ShapeDtypeStruct((wide // LANES,) + tile, F32), held, held),
            in_specs=[hbm, hbm, hbm],
            out_specs=[vmem] * 3,
            scratch_shapes=[pltpu.VMEM((RANK, units), F32), pltpu.SemaphoreType.DMA((3, steps))],
            compiler_params=params,
        )(*(pltpu.with_memory_space_constraint(x, pltpu.HBM) for x in (right_prior.T, gradient, feedback)))
    halves, mixed = plane_groups(replicas)
    members, reducers = len(halves[0]), len(mixed[0])
    share = (wide // LANES // members,) + tile
    with jax.named_scope("left_sum"):
        pieces = left.reshape((members,) + share)
        pieces = spread(lax.all_to_all(pieces, "tensor", 0, 0, axis_index_groups=halves), reducers)
        pieces = spread(lax.all_to_all(pieces, ("dp", "tensor"), 0, 0, axis_index_groups=mixed), members)
        left = lax.all_to_all(pieces, "tensor", 0, 0, axis_index_groups=halves)
        left = left.reshape((wide // LANES,) + tile)
    with jax.named_scope("right"):
        basis, right = pl.pallas_call(
            right_kernel,
            out_shape=(jax.ShapeDtypeStruct((6 * RANK, wide), BF16), jax.ShapeDtypeStruct((replicas, RANK, units), F32)),
            in_specs=[vmem, vmem, vmem],
            out_specs=[vmem, vmem],
            compiler_params=params,
        )(left, gradient, feedback)
    with jax.named_scope("right_sum"):
        rights = lax.all_to_all(right, "dp", 0, 0, axis_index_groups=[DP_ORDER])
    with jax.named_scope("rebuild"):
        update, residue, right_next = pl.pallas_call(
            functools.partial(rebuild_kernel, replicas),
            out_shape=(
                jax.ShapeDtypeStruct((units, CHUNK), BF16),
                jax.ShapeDtypeStruct((units, wide), BF16),
                jax.ShapeDtypeStruct((RANK, units), F32),
            ),
            in_specs=[vmem] * 4,
            out_specs=[hbm] * 3,
            scratch_shapes=[
                pltpu.VMEM((units, wide), BF16),
                pltpu.VMEM((units, CHUNK), BF16),
                pltpu.VMEM((RANK, units), F32),
                pltpu.SemaphoreType.DMA((steps + 2,)),
            ],
            compiler_params=params,
        )(rights, basis, gradient, feedback)
    return update.T, residue.T[None], right_next.T


def solution(mesh):
    placed = (P("dp", None, "tensor"), P("dp", None, "tensor"), P("tensor", None))
    return jax.shard_map(
        shards,
        mesh=mesh,
        in_specs=placed,
        out_specs=(P("dp", "tensor"), P("dp", None, "tensor"), P("tensor", None)),
        check_vma=False,
    )
```
